32 devices in a mesh: dp: 4 (over y, x), group: 8 (over z, core).
Axes of the slice: x: 2, y: 2, z: 4, core: 2. Of those that a mesh axis runs over, the one named last changes fastest.
Arguments:
- partials: bfloat16 [4, 4, 7168, 2048], P('dp', None, 'group'), may hold values from -25 to 25
- momentum: float32 [4, 7168, 2048], P('dp', 'group'), may hold values from -6 to 6
Outputs:
- momentum_out: float32 [4, 7168, 2048], P('dp', 'group')
- update: bfloat16 [4, 7168, 2048], P('dp', 'group')
The draws below stay inside these ranges and needn't reach their ends.
All inputs are finite; a program needn't handle non-finite values.
Results may differ from the reference program's by a relative error of at most 0.034.
Values may be sent and summed in bfloat16 or wider, within the bound.
A program may use at most 128 MiB of HBM per device.

```python
import math
import jax
import jax.numpy as jnp
from jax import lax

R = 2048
C = 7168
EXPERTS = 4
REPLICAS = 4


def draw_partials(key, part):
    key = jax.random.fold_in(key, 11)
    keys = jax.random.split(key, 3)
    shape = (REPLICAS, EXPERTS, C, R)
    base = jnp.clip(jax.random.normal(keys[0], shape, jnp.float32), -6.0, 6.0)
    span = math.log(10.0)
    low = 0.3
    rows = low * jnp.exp(jax.random.uniform(keys[1], (1, EXPERTS, 1, R), jnp.float32, 0.0, span))
    cols = low * jnp.exp(jax.random.uniform(keys[2], (1, EXPERTS, C, 1), jnp.float32, 0.0, span))
    return (0.35 * base * rows * cols).astype(jnp.bfloat16)


def shard_levels(key, dims, cuts, least, largest):
    def one(axis_at, parts):
        draws = jax.random.uniform(jax.random.fold_in(jax.random.fold_in(key, 6), axis_at), (parts,), jnp.float32, least / len(cuts), largest / len(cuts))
        return jnp.repeat(jnp.exp(draws), dims[axis_at] // parts).reshape((-1,) + (1,) * (len(dims) - axis_at - 1))

    gain = one(*cuts[0])
    for cut in cuts[1:]:
        gain = gain * one(*cut)
    return gain


def bell_draw(own_key, dims, width, most, pieces=(), held_as=jnp.bfloat16):
    level = shard_levels(own_key, dims, pieces, -0.22, 0.18) if pieces else 1.0
    drawn = jax.random.normal(own_key, dims, jnp.float32) * width * level
    return jnp.minimum(jnp.maximum(drawn, -most), most).astype(held_as)


def setup_inputs(seed: int = 0) -> dict:
    streams_of = jax.random.split(jax.random.key(seed), 3)
    return {
        "partials": draw_partials(jax.random.fold_in(streams_of[2], 71), 0),
        "momentum": bell_draw(streams_of[1], (EXPERTS, C, R), 1.0, 6.0, ((0, 4), (1, 8)), jnp.float32),
    }


def orthogonal(blend):
    xzero = blend.astype(jnp.bfloat16)
    wide = xzero.astype(jnp.float32)
    total = jnp.sum(wide * wide) + 1e-06
    scale2 = 2.0 * total / R
    gram = lax.dot_general(xzero, xzero, (((0,), (0,)), ((), ())), preferred_element_type=jnp.float32).astype(jnp.bfloat16)
    first = (lax.dot_general(xzero, gram, (((1,), (1,)), ((), ())), preferred_element_type=jnp.float32) / scale2).astype(jnp.bfloat16)
    second = lax.dot_general(first, gram, (((1,), (1,)), ((), ())), preferred_element_type=jnp.float32) / scale2
    ortho = (3.4445 * wide - 4.775 * first.astype(jnp.float32) + 2.0315 * second) / jnp.sqrt(scale2)
    return (ortho * math.sqrt(C)).astype(jnp.bfloat16)

def reference(partials, momentum):

    def one_expert(index):
        piece = lax.dynamic_index_in_dim(partials, index, 1, keepdims=False)
        grad = lax.optimization_barrier(jnp.sum(piece.astype(jnp.float32), axis=0))
        state = lax.dynamic_index_in_dim(momentum, index, 0, keepdims=False)
        state_new = 0.95 * state + grad
        blend = grad + 0.95 * state_new
        return (state_new, orthogonal(blend))
    momentum_out, update = lax.map(one_expert, jnp.arange(EXPERTS, dtype=jnp.int32))
    return (momentum_out, update)
```

```python
import functools
import math

import jax
import jax.numpy as jnp
from jax import lax
from jax.experimental import pallas as pl
from jax.experimental.pallas import tpu as pltpu
from jax.sharding import PartitionSpec as P

C = 7168
NB = 8
WINDOW = 2
MESH = pl.DeviceIdType.MESH


def orthogonal(block):
    rows_total = block.shape[1]
    gram_slab = lax.psum_scatter(
        lax.dot_general(
            block, block, (((0,), (0,)), ((), ())), preferred_element_type=jnp.float32
        ).astype(jnp.bfloat16),
        "group",
        scatter_dimension=0,
        tiled=True,
    )
    wide = block.astype(jnp.float32)
    total = lax.psum(jnp.sum(wide * wide), "group")
    gram_full = lax.all_gather(gram_slab, "group", axis=0, tiled=True)
    scale2 = 2.0 * (total + 1e-06) / rows_total
    first = (
        lax.dot_general(
            block, gram_full, (((1,), (1,)), ((), ())), preferred_element_type=jnp.float32
        )
        / scale2
    ).astype(jnp.bfloat16)
    second = (
        lax.dot_general(
            first, gram_full, (((1,), (1,)), ((), ())), preferred_element_type=jnp.float32
        )
        / scale2
    )
    ortho = (
        3.4445 * block.astype(jnp.float32) - 4.775 * first.astype(jnp.float32) + 2.0315 * second
    ) / jnp.sqrt(scale2)
    return (ortho * math.sqrt(C)).astype(jnp.bfloat16)


def shards(partials, momentum):
    grad = lax.psum_scatter(partials[0], "dp", scatter_dimension=0, tiled=True).astype(jnp.float32)
    momentum_out = 0.95 * momentum + grad
    blended = (grad + 0.95 * momentum_out).astype(jnp.bfloat16)
    results = [orthogonal(blended[0])]
    return (momentum_out, jnp.stack(results))


def sum_kernel(
    partials,
    momentum,
    mom_hbm,
    x_hbm,
    gram_hbm,
    via,
    near,
    far,
    relay_own,
    x,
    mom,
    xt,
    gram,
    part,
    pair_out,
    pair_in,
    chain,
    sums,
    load_sem,
    dp_send,
    dp_recv,
    pair_send,
    pair_recv,
    red_send,
    red_recv,
    bc_send,
    bc_recv,
    sib_send,
    sib_recv,
    store_sem,
):
    rows, cols = x.shape
    blk = cols // NB
    half = rows // 2
    dp = lax.axis_index("dp")
    group = lax.axis_index("group")
    y, xx = dp // 2, dp % 2
    z, core = group // 2, group % 2
    at_x, at_y, at_diag = y * 2 + (1 - xx), (1 - y) * 2 + xx, (1 - y) * 2 + (1 - xx)
    other = 1 - core
    sibling = (dp, z * 2 + other)

    barrier = pltpu.get_barrier_semaphore()
    for peer in (
        (at_x, group),
        (at_y, group),
        sibling,
        (dp, lax.rem(z + 1, 4) * 2 + core),
        (dp, lax.rem(z + 3, 4) * 2 + core),
    ):
        pl.semaphore_signal(barrier, inc=1, device_id=peer, device_id_type=MESH)
    pl.semaphore_wait(barrier, 5)

    span = [slice(0, half), slice(half, rows)]
    hop1 = [at_x, at_y]
    hop2 = [at_y, at_x]

    def col(k):
        return slice(k * blk, (k + 1) * blk)

    def dp_copy(kind, p, k):
        src, dst, to = (
            (partials.at[0, at_diag, span[p], col(k)], via, hop1[p]),
            (partials.at[0, hop1[p], span[p], col(k)], near, hop1[p]),
            (via.at[span[p], col(k)], far, hop2[p]),
        )[kind]
        return pltpu.make_async_remote_copy(
            src_ref=src,
            dst_ref=dst.at[span[p], col(k)],
            send_sem=dp_send.at[kind, p, k],
            recv_sem=dp_recv.at[kind, p, k],
            device_id=(to, group),
            device_id_type=MESH,
        )

    def loads(k):
        copies = [
            pltpu.make_async_copy(
                partials.at[0, hop2[p], span[p], col(k)],
                relay_own.at[span[p], col(k)],
                load_sem.at[p, k],
            )
            for p in range(2)
        ]
        copies.append(
            pltpu.make_async_copy(
                partials.at[0, dp, :, col(k)], x.at[:, col(k)], load_sem.at[2, k]
            )
        )
        copies.append(
            pltpu.make_async_copy(
                momentum.at[0, :, col(k)], mom.at[:, col(k)], load_sem.at[3, k]
            )
        )
        return copies

    def stores(k):
        top = (k + 1) * blk
        return [
            pltpu.make_async_copy(mom.at[:, col(k)], mom_hbm.at[:, col(k)], store_sem.at[0, k]),
            pltpu.make_async_copy(x.at[:, col(k)], x_hbm.at[:, col(k)], store_sem.at[1, k]),
            pltpu.make_async_copy(
                gram.at[0:top, col(k)], gram_hbm.at[0:top, col(k)], store_sem.at[2, k]
            ),
        ]

    def send_first(k):
        for kind in (0, 1):
            for p in range(2):
                dp_copy(kind, p, k).start()

    def forward(k):
        for p in range(2):
            dp_copy(0, p, k).wait_recv()
            loads(k)[p].wait()
            at = (span[p], col(k))
            via[at] = (
                via[at].astype(jnp.float32) + relay_own[at].astype(jnp.float32)
            ).astype(jnp.bfloat16)
            dp_copy(2, p, k).start()

    def unit(k):
        return (k + 1) * blk // 4

    def packed(k, h=None):
        start = blk // 4 * k * (k + 1)
        if h is None:
            return slice(start, start + 2 * unit(k))
        return slice(start + h * unit(k), start + (h + 1) * unit(k))

    def pair_copy(k):
        return pltpu.make_async_remote_copy(
            src_ref=pair_out.at[packed(k)],
            dst_ref=pair_in.at[packed(k)],
            send_sem=pair_send.at[k],
            recv_sem=pair_recv.at[k],
            device_id=sibling,
            device_id_type=MESH,
        )

    def blend(k):
        for copy in loads(k)[2:]:
            copy.wait()
        for kind in (1, 2):
            for p in range(2):
                dp_copy(kind, p, k).wait_recv()
        at = (slice(None), col(k))
        grad = (
            x[at].astype(jnp.float32) + near[at].astype(jnp.float32) + far[at].astype(jnp.float32)
        )
        state = 0.95 * mom[at] + grad
        mom[at] = state
        mixed = grad + 0.95 * state
        x[at] = mixed.astype(jnp.bfloat16)
        xt[col(k), :] = mixed.T.astype(jnp.bfloat16)
        for copy in stores(k)[:2]:
            copy.start()
        own = x[at]

        @pl.loop(0, k + 1)
        def _(r):
            strip = pl.ds(pl.multiple_of(r * blk, blk), blk)
            part[strip, :] = jnp.dot(xt[strip, :], own, preferred_element_type=jnp.float32)

        n = 2 * unit(k)
        pair_out[packed(k), :] = part[pl.ds(pl.multiple_of(other * n, n), n), :].astype(
            jnp.bfloat16
        )
        pair_copy(k).start()

    place = [z, 3 - z]

    def chip_at(h, spot):
        return spot if h == 0 else 3 - spot

    def final(k, h, owner):
        n = unit(k)
        return gram.at[pl.ds(pl.multiple_of(owner * 2 * n + h * n, n), n), col(k)]

    def red_copy(k, h, to_spot, slot):
        return pltpu.make_async_remote_copy(
            src_ref=sums.at[packed(k, h)],
            dst_ref=chain.at[slot, packed(k, h)],
            send_sem=red_send.at[h, k],
            recv_sem=red_recv.at[slot, h, k],
            device_id=(dp, chip_at(h, to_spot) * 2 + core),
            device_id_type=MESH,
        )

    def bc_copy(k, h, to_spot, slot):
        return pltpu.make_async_remote_copy(
            src_ref=final(k, h, core),
            dst_ref=final(k, h, core),
            send_sem=bc_send.at[slot, h, k],
            recv_sem=bc_recv.at[h, k],
            device_id=(dp, chip_at(h, to_spot) * 2 + core),
            device_id_type=MESH,
        )

    def sib_copy(k, h):
        return pltpu.make_async_remote_copy(
            src_ref=final(k, h, core),
            dst_ref=final(k, h, core),
            send_sem=sib_send.at[h, k],
            recv_sem=sib_recv.at[h, k],
            device_id=sibling,
            device_id_type=MESH,
        )

    def pair_sum(k):
        pair_copy(k).wait_recv()
        n = 2 * unit(k)
        sums[packed(k), :] = (
            part[pl.ds(pl.multiple_of(core * n, n), n), :]
            + pair_in[packed(k), :].astype(jnp.float32)
        ).astype(jnp.bfloat16)
        for h in range(2):

            @pl.when(place[h] == 0)
            def _():
                red_copy(k, h, 1, 0).start()

            @pl.when(place[h] == 3)
            def _():
                red_copy(k, h, 2, 0).start()

    def relay(k):
        for h in range(2):

            @pl.when(place[h] == 2)
            def _():
                at = packed(k, h)
                red_copy(k, h, 2, 0).wait_recv()
                sums[at, :] = (
                    sums[at, :].astype(jnp.float32) + chain[0, at, :].astype(jnp.float32)
                ).astype(jnp.bfloat16)
                red_copy(k, h, 1, 1).start()

    def root(k):
        for h in range(2):

            @pl.when(place[h] == 1)
            def _():
                at = packed(k, h)
                red_copy(k, h, 1, 0).wait_recv()
                red_copy(k, h, 1, 1).wait_recv()
                final(k, h, core)[...] = (
                    sums[at, :].astype(jnp.float32)
                    + chain[0, at, :].astype(jnp.float32)
                    + chain[1, at, :].astype(jnp.float32)
                ).astype(jnp.bfloat16)
                bc_copy(k, h, 2, 1).start()
                bc_copy(k, h, 0, 0).start()
                sib_copy(k, h).start()

    def spread(k):
        for h in range(2):

            @pl.when(place[h] == 2)
            def _():
                bc_copy(k, h, 2, 1).wait_recv()
                bc_copy(k, h, 3, 0).start()
                sib_copy(k, h).start()

    def leaf(k):
        for h in range(2):

            @pl.when((place[h] == 0) | (place[h] == 3))
            def _():
                bc_copy(k, h, 0, 0).wait_recv()
                sib_copy(k, h).start()

    def finish(k):
        for h in range(2):
            sib_copy(k, h).wait_recv()
        stores(k)[2].start()

    for k in range(WINDOW):
        send_first(k)
    for k in range(NB):
        for copy in loads(k):
            copy.start()

    stages = (
        (0, forward),
        (0, lambda k: send_first(k + WINDOW) if k + WINDOW < NB else None),
        (4, spread),
        (5, leaf),
        (6, finish),
        (2, blend),
        (3, relay),
        (2, pair_sum),
        (3, root),
    )
    for step in range(NB + 6):
        for lag, stage in stages:
            if 0 <= step - lag < NB:
                stage(step - lag)

    for k in range(NB):
        for copy in stores(k):
            copy.wait()
        for p in range(2):
            for kind in range(3):
                dp_copy(kind, p, k).wait_send()
        pair_copy(k).wait_send()
        for h in range(2):
            sib_copy(k, h).wait_send()

            @pl.when(place[h] != 1)
            def _():
                red_copy(k, h, 1, 0).wait_send()

            @pl.when((place[h] == 1) | (place[h] == 2))
            def _():
                bc_copy(k, h, 0, 0).wait_send()

            @pl.when(place[h] == 1)
            def _():
                bc_copy(k, h, 2, 1).wait_send()


def finish_kernel(x_ref, gram_ref, mom_ref, mom_out, update, first):
    cols = x_ref.shape[1]
    blk = cols // NB
    mom_out[...] = mom_ref[...]
    eye = lax.broadcasted_iota(jnp.int32, (blk, blk), 0) == lax.broadcasted_iota(
        jnp.int32, (blk, blk), 1
    )
    trace = jnp.zeros((blk, blk), jnp.float32)
    for k in range(NB):
        at = slice(k * blk, (k + 1) * blk)
        trace += jnp.where(eye, gram_ref[at, at].astype(jnp.float32), 0.0)
    total = jnp.sum(trace) + 1e-06
    scale2 = jnp.full((1, blk), 2.0 / cols, jnp.float32) * total
    inv = 1.0 / scale2
    last = lax.rsqrt(scale2) * math.sqrt(C)

    def times_gram(left, k):
        at, split = slice(k * blk, (k + 1) * blk), (k + 1) * blk
        acc = jnp.dot(
            left[:, :split], gram_ref[:split, at], preferred_element_type=jnp.float32
        )
        if split < cols:
            acc += lax.dot_general(
                left[:, split:],
                gram_ref[at, split:],
                (((1,), (1,)), ((), ())),
                preferred_element_type=jnp.float32,
            )
        return acc

    for k in range(NB):
        first[:, k * blk : (k + 1) * blk] = (times_gram(x_ref, k) * inv).astype(jnp.bfloat16)
    for k in range(NB):
        at = slice(k * blk, (k + 1) * blk)
        second = times_gram(first, k) * inv
        ortho = (
            3.4445 * x_ref[:, at].astype(jnp.float32)
            - 4.775 * first[:, at].astype(jnp.float32)
            + 2.0315 * second
        )
        update[:, at] = (ortho * last).astype(jnp.bfloat16)


def kernels(partials, momentum):
    _, _, rows, cols = partials.shape
    blk = cols // NB
    packed_rows = blk // 4 * NB * (NB + 1)
    bf16, f32 = jnp.bfloat16, jnp.float32
    dma = pltpu.SemaphoreType.DMA
    mom_new, x, gram = pl.pallas_call(
        sum_kernel,
        out_shape=(
            jax.ShapeDtypeStruct((rows, cols), f32),
            jax.ShapeDtypeStruct((rows, cols), bf16),
            jax.ShapeDtypeStruct((cols, cols), bf16),
        ),
        in_specs=[pl.BlockSpec(memory_space=pl.ANY)] * 2,
        out_specs=[pl.BlockSpec(memory_space=pl.ANY)] * 3,
        scratch_shapes=[
            pltpu.VMEM((rows, cols), bf16),
            pltpu.VMEM((rows, cols), bf16),
            pltpu.VMEM((rows, cols), bf16),
            pltpu.VMEM((rows, cols), bf16),
            pltpu.VMEM((rows, cols), bf16),
            pltpu.VMEM((rows, cols), f32),
            pltpu.VMEM((cols, rows), bf16),
            pltpu.VMEM((cols, cols), bf16),
            pltpu.VMEM((cols, blk), f32),
            pltpu.VMEM((packed_rows, blk), bf16),
            pltpu.VMEM((packed_rows, blk), bf16),
            pltpu.VMEM((2, packed_rows, blk), bf16),
            pltpu.VMEM((packed_rows, blk), bf16),
            dma((4, NB)),
            dma((3, 2, NB)),
            dma((3, 2, NB)),
            dma((NB,)),
            dma((NB,)),
            dma((2, NB)),
            dma((2, 2, NB)),
            dma((2, 2, NB)),
            dma((2, NB)),
            dma((2, NB)),
            dma((2, NB)),
            dma((3, NB)),
        ],
        compiler_params=pltpu.CompilerParams(
            collective_id=0, has_side_effects=True, vmem_limit_bytes=60 * 2**20
        ),
        name="sum_and_gram",
    )(partials, momentum)
    tile = rows // 2
    momentum_out, update = pl.pallas_call(
        finish_kernel,
        grid=(rows // tile,),
        out_shape=(
            jax.ShapeDtypeStruct((rows, cols), f32),
            jax.ShapeDtypeStruct((rows, cols), bf16),
        ),
        in_specs=[
            pl.BlockSpec((tile, cols), lambda i: (i, 0)),
            pl.BlockSpec((cols, cols), lambda i: (0, 0), pipeline_mode=pl.Buffered(1)),
            pl.BlockSpec((tile, cols), lambda i: (i, 0)),
        ],
        out_specs=[
            pl.BlockSpec((tile, cols), lambda i: (i, 0)),
            pl.BlockSpec((tile, cols), lambda i: (i, 0)),
        ],
        scratch_shapes=[pltpu.VMEM((tile, cols), bf16)],
        compiler_params=pltpu.CompilerParams(vmem_limit_bytes=60 * 2**20),
        name="newton_schulz",
    )(x, gram, mom_new)
    return momentum_out[None], update[None]


def solution(mesh):
    fits = mesh.shape["dp"] == 4 and mesh.shape["group"] == 8
    return jax.shard_map(
        kernels if fits else shards,
        mesh=mesh,
        in_specs=(P("dp", None, "group", None), P("dp", "group", None)),
        out_specs=(P("dp", "group", None), P("dp", "group", None)),
        check_vma=False,
    )
```

```python
import functools
import math

import jax
import jax.numpy as jnp
from jax import lax
from jax.experimental import pallas as pl
from jax.experimental.pallas import tpu as pltpu
from jax.sharding import PartitionSpec as P

C = 7168
EDGES = (0, 2, 4, 6, 8, 10, 12, 14, 15, 16)
NB = len(EDGES) - 1
WINDOW = 2
MESH = pl.DeviceIdType.MESH


def orthogonal(block):
    rows_total = block.shape[1]
    gram_slab = lax.psum_scatter(
        lax.dot_general(
            block, block, (((0,), (0,)), ((), ())), preferred_element_type=jnp.float32
        ).astype(jnp.bfloat16),
        "group",
        scatter_dimension=0,
        tiled=True,
    )
    wide = block.astype(jnp.float32)
    total = lax.psum(jnp.sum(wide * wide), "group")
    gram_full = lax.all_gather(gram_slab, "group", axis=0, tiled=True)
    scale2 = 2.0 * (total + 1e-06) / rows_total
    first = (
        lax.dot_general(
            block, gram_full, (((1,), (1,)), ((), ())), preferred_element_type=jnp.float32
        )
        / scale2
    ).astype(jnp.bfloat16)
    second = (
        lax.dot_general(
            first, gram_full, (((1,), (1,)), ((), ())), preferred_element_type=jnp.float32
        )
        / scale2
    )
    ortho = (
        3.4445 * block.astype(jnp.float32) - 4.775 * first.astype(jnp.float32) + 2.0315 * second
    ) / jnp.sqrt(scale2)
    return (ortho * math.sqrt(C)).astype(jnp.bfloat16)


def shards(partials, momentum):
    grad = lax.psum_scatter(partials[0], "dp", scatter_dimension=0, tiled=True).astype(jnp.float32)
    momentum_out = 0.95 * momentum + grad
    blended = (grad + 0.95 * momentum_out).astype(jnp.bfloat16)
    results = [orthogonal(blended[0])]
    return (momentum_out, jnp.stack(results))


def times_gram(left, gram, edge, k, low, high):
    at, split = slice(edge[k], edge[k + 1]), edge[k + 1]
    acc = None
    if low < split:
        acc = jnp.dot(
            left[:, low : min(split, high)],
            gram[low : min(split, high), at],
            preferred_element_type=jnp.float32,
        )
    if split < high:
        start = max(split, low)
        more = lax.dot_general(
            left[:, start:high],
            gram[at, start:high],
            (((1,), (1,)), ((), ())),
            preferred_element_type=jnp.float32,
        )
        acc = more if acc is None else acc + more
    return acc


def sum_kernel(
    partials,
    momentum,
    mom_hbm,
    x_hbm,
    gram_hbm,
    via,
    near,
    far,
    relay_own,
    x,
    mom,
    xt,
    gram,
    part,
    pair_out,
    pair_in,
    chain,
    sums,
    load_sem,
    dp_send,
    dp_recv,
    pair_send,
    pair_recv,
    red_send,
    red_recv,
    bc_send,
    bc_recv,
    sib_send,
    sib_recv,
    store_sem,
):
    rows, cols = x.shape
    wide = cols // 8
    edge = [e * cols // 16 for e in EDGES]
    half = rows // 2
    dp = lax.axis_index("dp")
    group = lax.axis_index("group")
    y, xx = dp // 2, dp % 2
    z, core = group // 2, group % 2
    at_x, at_y, at_diag = y * 2 + (1 - xx), (1 - y) * 2 + xx, (1 - y) * 2 + (1 - xx)
    other = 1 - core
    sibling = (dp, z * 2 + other)

    barrier = pltpu.get_barrier_semaphore()
    for peer in (
        (at_x, group),
        (at_y, group),
        sibling,
        (dp, lax.rem(z + 1, 4) * 2 + core),
        (dp, lax.rem(z + 3, 4) * 2 + core),
    ):
        pl.semaphore_signal(barrier, inc=1, device_id=peer, device_id_type=MESH)
    pl.semaphore_wait(barrier, 5)

    span = [slice(0, half), slice(half, rows)]
    hop1 = [at_x, at_y]
    hop2 = [at_y, at_x]

    def col(k):
        return slice(edge[k], edge[k + 1])

    def dp_copy(kind, p, k):
        src, dst, to = (
            (partials.at[0, at_diag, span[p], col(k)], via, hop1[p]),
            (partials.at[0, hop1[p], span[p], col(k)], near, hop1[p]),
            (via.at[span[p], col(k)], far, hop2[p]),
        )[kind]
        return pltpu.make_async_remote_copy(
            src_ref=src,
            dst_ref=dst.at[span[p], col(k)],
            send_sem=dp_send.at[kind, p, k],
            recv_sem=dp_recv.at[kind, p, k],
            device_id=(to, group),
            device_id_type=MESH,
        )

    def loads(k):
        copies = [
            pltpu.make_async_copy(
                partials.at[0, hop2[p], span[p], col(k)],
                relay_own.at[span[p], col(k)],
                load_sem.at[p, k],
            )
            for p in range(2)
        ]
        copies.append(
            pltpu.make_async_copy(
                partials.at[0, dp, :, col(k)], x.at[:, col(k)], load_sem.at[2, k]
            )
        )
        copies.append(
            pltpu.make_async_copy(
                momentum.at[0, :, col(k)], mom.at[:, col(k)], load_sem.at[3, k]
            )
        )
        return copies

    def stores(k):
        top = edge[k + 1]
        return [
            pltpu.make_async_copy(mom.at[:, col(k)], mom_hbm.at[:, col(k)], store_sem.at[0, k]),
            pltpu.make_async_copy(x.at[:, col(k)], x_hbm.at[:, col(k)], store_sem.at[1, k]),
            pltpu.make_async_copy(
                gram.at[0:top, col(k)], gram_hbm.at[0:top, col(k)], store_sem.at[2, k]
            ),
        ]

    def send_first(k):
        for kind in (0, 1):
            for p in range(2):
                dp_copy(kind, p, k).start()

    def forward(k):
        for p in range(2):
            dp_copy(0, p, k).wait_recv()
            loads(k)[p].wait()
            at = (span[p], col(k))
            via[at] = (
                via[at].astype(jnp.float32) + relay_own[at].astype(jnp.float32)
            ).astype(jnp.bfloat16)
            dp_copy(2, p, k).start()

    def unit(k):
        return edge[k + 1] // 4

    def packed(k, h=None):
        start = sum(2 * unit(i) for i in range(k))
        across = slice(0, edge[k + 1] - edge[k])
        if h is None:
            return slice(start, start + 2 * unit(k)), across
        return slice(start + h * unit(k), start + (h + 1) * unit(k)), across

    def pair_copy(k):
        return pltpu.make_async_remote_copy(
            src_ref=pair_out.at[packed(k)],
            dst_ref=pair_in.at[packed(k)],
            send_sem=pair_send.at[k],
            recv_sem=pair_recv.at[k],
            device_id=sibling,
            device_id_type=MESH,
        )

    def blend(k):
        for copy in loads(k)[2:]:
            copy.wait()
        for kind in (1, 2):
            for p in range(2):
                dp_copy(kind, p, k).wait_recv()
        at = (slice(None), col(k))
        grad = (
            x[at].astype(jnp.float32) + near[at].astype(jnp.float32) + far[at].astype(jnp.float32)
        )
        state = 0.95 * mom[at] + grad
        mom[at] = state
        mixed = grad + 0.95 * state
        x[at] = mixed.astype(jnp.bfloat16)
        xt[col(k), :] = mixed.T.astype(jnp.bfloat16)
        for copy in stores(k)[:2]:
            copy.start()
        own = x[at]

        width = edge[k + 1] - edge[k]

        def strip(at):
            part[at, :width] = jnp.dot(xt[at, :], own, preferred_element_type=jnp.float32)

        whole = edge[k + 1] // wide

        @pl.loop(0, whole)
        def _(r):
            strip(pl.ds(pl.multiple_of(r * wide, wide), wide))

        if whole * wide < edge[k + 1]:
            strip(slice(whole * wide, edge[k + 1]))

        n = 2 * unit(k)
        pair_out[packed(k)] = part[pl.ds(pl.multiple_of(other * n, n), n), :width].astype(
            jnp.bfloat16
        )
        pair_copy(k).start()

    place = [z, 3 - z]

    def chip_at(h, spot):
        return spot if h == 0 else 3 - spot

    def final(k, h, owner):
        n = unit(k)
        return gram.at[pl.ds(pl.multiple_of(owner * 2 * n + h * n, n), n), col(k)]

    def red_copy(k, h, to_spot, slot):
        return pltpu.make_async_remote_copy(
            src_ref=sums.at[packed(k, h)],
            dst_ref=chain.at[(slot, *packed(k, h))],
            send_sem=red_send.at[h, k],
            recv_sem=red_recv.at[slot, h, k],
            device_id=(dp, chip_at(h, to_spot) * 2 + core),
            device_id_type=MESH,
        )

    def bc_copy(k, h, to_spot, slot):
        return pltpu.make_async_remote_copy(
            src_ref=final(k, h, core),
            dst_ref=final(k, h, core),
            send_sem=bc_send.at[slot, h, k],
            recv_sem=bc_recv.at[h, k],
            device_id=(dp, chip_at(h, to_spot) * 2 + core),
            device_id_type=MESH,
        )

    def sib_copy(k, h):
        return pltpu.make_async_remote_copy(
            src_ref=final(k, h, core),
            dst_ref=final(k, h, core),
            send_sem=sib_send.at[h, k],
            recv_sem=sib_recv.at[h, k],
            device_id=sibling,
            device_id_type=MESH,
        )

    def pair_sum(k):
        pair_copy(k).wait_recv()
        n = 2 * unit(k)
        sums[packed(k)] = (
            part[pl.ds(pl.multiple_of(core * n, n), n), : edge[k + 1] - edge[k]]
            + pair_in[packed(k)].astype(jnp.float32)
        ).astype(jnp.bfloat16)
        for h in range(2):

            @pl.when(place[h] == 0)
            def _():
                red_copy(k, h, 1, 0).start()

            @pl.when(place[h] == 3)
            def _():
                red_copy(k, h, 2, 0).start()

    def relay(k):
        for h in range(2):

            @pl.when(place[h] == 2)
            def _():
                at = packed(k, h)
                red_copy(k, h, 2, 0).wait_recv()
                sums[at] = (
                    sums[at].astype(jnp.float32) + chain[(0, *at)].astype(jnp.float32)
                ).astype(jnp.bfloat16)
                red_copy(k, h, 1, 1).start()

    def root(k):
        for h in range(2):

            @pl.when(place[h] == 1)
            def _():
                at = packed(k, h)
                red_copy(k, h, 1, 0).wait_recv()
                red_copy(k, h, 1, 1).wait_recv()
                final(k, h, core)[...] = (
                    sums[at].astype(jnp.float32)
                    + chain[(0, *at)].astype(jnp.float32)
                    + chain[(1, *at)].astype(jnp.float32)
                ).astype(jnp.bfloat16)
                bc_copy(k, h, 2, 1).start()
                bc_copy(k, h, 0, 0).start()
                sib_copy(k, h).start()

    def spread(k):
        for h in range(2):

            @pl.when(place[h] == 2)
            def _():
                bc_copy(k, h, 2, 1).wait_recv()
                bc_copy(k, h, 3, 0).start()
                sib_copy(k, h).start()

    def leaf(k):
        for h in range(2):

            @pl.when((place[h] == 0) | (place[h] == 3))
            def _():
                bc_copy(k, h, 0, 0).wait_recv()
                sib_copy(k, h).start()

    def finish(k):
        for h in range(2):
            sib_copy(k, h).wait_recv()
        stores(k)[2].start()

    for k in range(WINDOW):
        send_first(k)
    for k in range(NB):
        for copy in loads(k):
            copy.start()

    stages = (
        (0, forward),
        (0, lambda k: send_first(k + WINDOW) if k + WINDOW < NB else None),
        (3, pair_sum),
        (4, root),
        (6, finish),
        (2, blend),
        (3, relay),
        (4, spread),
        (5, leaf),
    )
    for step in range(NB + 2):
        for lag, stage in stages:
            if 0 <= step - lag < NB:
                stage(step - lag)
    end = NB - 1
    pair_sum(end)
    root(end - 1)
    spread(end - 1)
    leaf(end - 2)
    finish(end - 3)
    finish(end - 2)
    relay(end)
    root(end)
    spread(end)
    leaf(end - 1)
    leaf(end)
    finish(end - 1)
    finish(end)

    for k in range(NB):
        for copy in stores(k):
            copy.wait()
        for p in range(2):
            for kind in range(3):
                dp_copy(kind, p, k).wait_send()
        pair_copy(k).wait_send()
        for h in range(2):
            sib_copy(k, h).wait_send()

            @pl.when(place[h] != 1)
            def _():
                red_copy(k, h, 1, 0).wait_send()

            @pl.when((place[h] == 1) | (place[h] == 2))
            def _():
                bc_copy(k, h, 0, 0).wait_send()

            @pl.when(place[h] == 1)
            def _():
                bc_copy(k, h, 2, 1).wait_send()


def finish_kernel(x_ref, gram_ref, mom_ref, mom_out, update, first):
    cols = x_ref.shape[1]
    edge = [e * cols // 16 for e in EDGES]
    mom_out[...] = mom_ref[...]
    trace = jnp.zeros((1, 1), jnp.float32)
    for k in range(NB):
        at, w = slice(edge[k], edge[k + 1]), edge[k + 1] - edge[k]
        eye = lax.broadcasted_iota(jnp.int32, (w, w), 0) == lax.broadcasted_iota(
            jnp.int32, (w, w), 1
        )
        corner = jnp.where(eye, gram_ref[at, at].astype(jnp.float32), 0.0)
        trace += jnp.sum(jnp.sum(corner, axis=0, keepdims=True), axis=1, keepdims=True)
    scale2 = (trace + 1e-06) * (2.0 / cols)
    inv = 1.0 / scale2
    last = lax.rsqrt(scale2) * math.sqrt(C)

    for k in range(NB):
        at = slice(edge[k], edge[k + 1])
        first[:, at] = (times_gram(x_ref, gram_ref, edge, k, 0, cols) * inv).astype(jnp.bfloat16)
    for k in range(NB):
        at = slice(edge[k], edge[k + 1])
        second = times_gram(first, gram_ref, edge, k, 0, cols) * inv
        ortho = (
            3.4445 * x_ref[:, at].astype(jnp.float32)
            - 4.775 * first[:, at].astype(jnp.float32)
            + 2.0315 * second
        )
        update[:, at] = (ortho * last).astype(jnp.bfloat16)


def kernels(partials, momentum):
    _, _, rows, cols = partials.shape
    blk = cols // 8
    packed_rows = sum(e * cols // 32 for e in EDGES)
    bf16, f32 = jnp.bfloat16, jnp.float32
    dma = pltpu.SemaphoreType.DMA
    mom_new, x, gram = pl.pallas_call(
        sum_kernel,
        out_shape=(
            jax.ShapeDtypeStruct((rows, cols), f32),
            jax.ShapeDtypeStruct((rows, cols), bf16),
            jax.ShapeDtypeStruct((cols, cols), bf16),
        ),
        in_specs=[pl.BlockSpec(memory_space=pl.ANY)] * 2,
        out_specs=[pl.BlockSpec(memory_space=pl.ANY)] * 3,
        scratch_shapes=[
            pltpu.VMEM((rows, cols), bf16),
            pltpu.VMEM((rows, cols), bf16),
            pltpu.VMEM((rows, cols), bf16),
            pltpu.VMEM((rows, cols), bf16),
            pltpu.VMEM((rows, cols), bf16),
            pltpu.VMEM((rows, cols), f32),
            pltpu.VMEM((cols, rows), bf16),
            pltpu.VMEM((cols, cols), bf16),
            pltpu.VMEM((cols, blk), f32),
            pltpu.VMEM((packed_rows, blk), bf16),
            pltpu.VMEM((packed_rows, blk), bf16),
            pltpu.VMEM((2, packed_rows, blk), bf16),
            pltpu.VMEM((packed_rows, blk), bf16),
            dma((4, NB)),
            dma((3, 2, NB)),
            dma((3, 2, NB)),
            dma((NB,)),
            dma((NB,)),
            dma((2, NB)),
            dma((2, 2, NB)),
            dma((2, 2, NB)),
            dma((2, NB)),
            dma((2, NB)),
            dma((2, NB)),
            dma((3, NB)),
        ],
        compiler_params=pltpu.CompilerParams(
            collective_id=0, has_side_effects=True, vmem_limit_bytes=60 * 2**20
        ),
        name="sum_and_gram",
    )(partials, momentum)
    tile = rows // 2
    momentum_out, update = pl.pallas_call(
        finish_kernel,
        grid=(rows // tile,),
        out_shape=(
            jax.ShapeDtypeStruct((rows, cols), f32),
            jax.ShapeDtypeStruct((rows, cols), bf16),
        ),
        in_specs=[
            pl.BlockSpec((tile, cols), lambda i: (i, 0)),
            pl.BlockSpec((cols, cols), lambda i: (0, 0), pipeline_mode=pl.Buffered(1)),
            pl.BlockSpec((tile, cols), lambda i: (i, 0)),
        ],
        out_specs=[
            pl.BlockSpec((tile, cols), lambda i: (i, 0)),
            pl.BlockSpec((tile, cols), lambda i: (i, 0)),
        ],
        scratch_shapes=[pltpu.VMEM((tile, cols), bf16)],
        compiler_params=pltpu.CompilerParams(vmem_limit_bytes=60 * 2**20),
        name="newton_schulz",
    )(x, gram, mom_new)
    return momentum_out[None], update[None]


def solution(mesh):
    fits = mesh.shape["dp"] == 4 and mesh.shape["group"] == 8
    return jax.shard_map(
        kernels if fits else shards,
        mesh=mesh,
        in_specs=(P("dp", None, "group", None), P("dp", "group", None)),
        out_specs=(P("dp", "group", None), P("dp", "group", None)),
        check_vma=False,
    )
```
